512 devices in a mesh: grp: 8 (over x, core), row: 4 (over z_hi), col: 16 (over z_lo, y).
Axes of the slice: x: 4, y: 4, z: 16 (z_hi: 4, z_lo: 4; z = z_hi * 4 + z_lo), core: 2. Of those that a mesh axis runs over, the one named last changes fastest.
Arguments:
- s_parent: float32 [15360, 15360], P(('row', 'col'), 'grp'), may hold values from -12 to 12
- child_factor: float32 [15360, 1024], P(('grp', 'row', 'col')), may hold values from -0.046875 to 0.046875
- panel_inverse: float32 [2, 512, 512], replicated, may hold values from -1 to 1, as said below
- pivot_kind: int32 [2, 512], replicated, may hold values from 0 to 2, as said below
- pivot_diag: float32 [2, 512], replicated, may hold values from -2 to 2, as said below
- pivot_couple: float32 [2, 512], replicated, may hold values from -4 to 4, as said below
- child_mask: int32 [2, 15360], replicated, may hold values 0 or 1
Outputs:
- off_inverse: float32 [15360, 1024], P(('row', 'col'), 'grp')
- diag_inverse: float32 [512, 1024], P(None, 'grp')
The draws below stay inside these ranges and needn't reach their ends.
Inputs may be any that keep to these rules, and one draw needn't show every extreme that they name: `panel_inverse`: unit lower triangular. `pivot_kind`: 0 marks a 1x1 pivot, 1 and 2 the first and second column of a 2x2 pivot; 2x2 pivots occupy column pairs 2i, 2i + 1. `pivot_diag`: magnitudes from 0.5 to 2. `pivot_couple`: magnitudes from 3 to 4.
All inputs are finite; a program needn't handle non-finite values.
Results may differ from the reference program's by a relative error of at most 0.00011.
Values sent between devices are 32-bit elements; how exact they have to be, the bound alone decides.
No kernel may reach another device: no remote copies, remote signals or barrier semaphores. Data moves between devices by JAX's collectives and lax.ppermute only.
A program may use at most 64 MiB of HBM per device.

```python
import math
import jax
import jax.numpy as jnp
from jax import lax

P_SIZE = 15360
C = 512
G = 2


def draw_s_parent(key, part):
    key = jax.random.fold_in(key, 11)
    values = jnp.clip(jax.random.normal(key, (P_SIZE, P_SIZE), jnp.float32), -8.0, 8.0)
    return (values + values.T) * 0.7071


def draw_panel_inverse(key, part):
    key = jax.random.fold_in(key, 12)
    strict_part = jnp.clip(jax.random.normal(key, (G, C, C), jnp.float32), -6.0, 6.0) * (1.0 / math.sqrt(C))
    row_ids = jnp.arange(C)[:, None]
    col_ids = jnp.arange(C)[None, :]
    unit_part = jnp.where(row_ids == col_ids, 1.0, 0.0).astype(jnp.float32)
    return jnp.where(row_ids > col_ids, strict_part, 0.0) + unit_part


def draw_pivot_kind(key, part):
    key = jax.random.fold_in(key, 13)
    paired = jax.random.randint(key, (G, C // 2), 0, 2)
    return jnp.stack([paired, paired * 2], axis=-1).reshape(G, C).astype(jnp.int32)


def draw_pivot_diag(key, part):
    key = jax.random.fold_in(key, 14)
    sign_key, size_key = jax.random.split(key)
    sign_part = jnp.where(jax.random.randint(sign_key, (G, C), 0, 2) == 0, -1.0, 1.0)
    magnitude = jnp.exp(jax.random.uniform(size_key, (G, C), jnp.float32, math.log(0.5), math.log(2.0)))
    return (sign_part * magnitude).astype(jnp.float32)


def draw_pivot_couple(key, part):
    key = jax.random.fold_in(key, 15)
    sign_key, size_key = jax.random.split(key)
    sign_part = jnp.where(jax.random.randint(sign_key, (G, C), 0, 2) == 0, -1.0, 1.0)
    magnitude = jax.random.uniform(size_key, (G, C), jnp.float32, 3.0, 4.0)
    return (sign_part * magnitude).astype(jnp.float32)


def set_ends(values, rng, smallest, largest):
    index_at = [jax.random.randint(jax.random.fold_in(rng, axis), (), 0, length) for axis, length in enumerate(values.shape)]
    longest = values.shape.index(max(values.shape))
    neighbour = index_at[:longest] + [(index_at[longest] + 1) % values.shape[longest]] + index_at[longest + 1:]
    return values.at[tuple(index_at)].set(smallest).at[tuple(neighbour)].set(largest)


def block_levels(rng, dims, cuts, low, high):
    factor_of, own = 1.0, jax.random.fold_in(rng, 6)
    for dim, shards_of in cuts:
        heights = jnp.exp(jax.random.uniform(jax.random.fold_in(own, dim), (shards_of,), jnp.float32, low / len(cuts), high / len(cuts)))
        factor_of = factor_of * jnp.repeat(heights, dims[dim] // shards_of).reshape([-1 if axis == dim else 1 for axis in range(len(dims))])
    return factor_of


def gaussian(key, extent, scale, limit, pieces=(), held_as=jnp.bfloat16):
    loudness = block_levels(key, extent, pieces, -0.22, 0.18) if pieces else 1.0
    result = jax.random.normal(key, extent, jnp.float32) * scale * loudness
    return jnp.minimum(jnp.maximum(result, -limit), limit).astype(held_as)


def setup_inputs(seed: int = 0) -> dict:
    streams_of = jax.random.split(jax.random.key(seed), 8)
    return {
        "s_parent": draw_s_parent(jax.random.fold_in(streams_of[7], 71), 0),
        "child_factor": gaussian(streams_of[1], (P_SIZE, G * C), P_SIZE ** -0.5, 0.046875, ((0, 512),), jnp.float32),
        "panel_inverse": draw_panel_inverse(jax.random.fold_in(streams_of[7], 71), 0),
        "pivot_kind": draw_pivot_kind(jax.random.fold_in(streams_of[7], 71), 0),
        "pivot_diag": draw_pivot_diag(jax.random.fold_in(streams_of[7], 71), 0),
        "pivot_couple": draw_pivot_couple(jax.random.fold_in(streams_of[7], 71), 0),
        "child_mask": set_ends((jax.random.randint(streams_of[6], (G, P_SIZE), 0, 4) < 3).astype(jnp.int32), jax.random.fold_in(streams_of[6], 1), 0, 1),
    }


highest = lax.Precision.HIGHEST


def pivot_solve(inverse, pivot_kind, pivot_diag, pivot_couple):
    diag_next = jnp.roll(pivot_diag, -1)
    diag_prev = jnp.roll(pivot_diag, 1)
    couple_prev = jnp.roll(pivot_couple, 1)
    det_here = pivot_diag * diag_next - pivot_couple * pivot_couple
    det_prev = diag_prev * pivot_diag - couple_prev * couple_prev
    self_coef = jnp.where(pivot_kind == 0, 1.0 / pivot_diag, jnp.where(pivot_kind == 1, diag_next / det_here, diag_prev / det_prev))
    next_coef = jnp.where(pivot_kind == 1, -pivot_couple / det_here, 0.0)
    prev_coef = jnp.where(pivot_kind == 2, -couple_prev / det_prev, 0.0)
    inv_next = jnp.roll(inverse, -1, axis=0)
    inv_prev = jnp.roll(inverse, 1, axis=0)
    return self_coef[:, None] * inverse + next_coef[:, None] * inv_next + prev_coef[:, None] * inv_prev


def reference(s_parent, child_factor, panel_inverse, pivot_kind, pivot_diag, pivot_couple, child_mask):
    rows_list = []
    weight_list = []
    for branch in range(G):
        weights = child_mask[branch].astype(jnp.float32)
        factor = child_factor[:, branch * C:(branch + 1) * C]
        rows_list.append(jnp.dot(weights[:, None] * factor, panel_inverse[branch], precision=highest, preferred_element_type=jnp.float32))
        weight_list.append(weights)
    rows_y = jnp.concatenate(rows_list, axis=1)
    parent_image = jnp.dot(s_parent, rows_y, precision=highest, preferred_element_type=jnp.float32)
    off_blocks = []
    panels = []
    for branch in range(G):
        masked = weight_list[branch][:, None] * parent_image[:, branch * C:(branch + 1) * C]
        off_blocks.append(-masked)
        inverse = panel_inverse[branch]
        scaled = pivot_solve(inverse, pivot_kind[branch], pivot_diag[branch], pivot_couple[branch])
        first_term = jnp.dot(inverse.T, scaled, precision=highest, preferred_element_type=jnp.float32)
        second_term = jnp.dot(rows_list[branch].T, masked, precision=highest, preferred_element_type=jnp.float32)
        panels.append(first_term + second_term)
    return jnp.concatenate(off_blocks, axis=1), jnp.concatenate(panels, axis=1)
```

```python
import functools

import jax
import jax.numpy as jnp
import numpy as np
from jax import lax
from jax.experimental import pallas as pl
from jax.experimental.pallas import tpu as pltpu
from jax.sharding import Mesh
from jax.sharding import PartitionSpec as P

f32, bf16 = jnp.float32, jnp.bfloat16
highest = lax.Precision.HIGHEST

AXES = ("x", "c", "h", "l", "y")
Z = ("h", "l")
GRP = ("x", "c")
PLANE = ("x", "c", "y")
NZ, NY, NG = 16, 4, 8
SHARD = 30
SLOT = 32
ROWS = 240
PAD = 256
HALF = PAD // 2
COLS = 1920
WIDE = 1024
C = 512
OWN = 128
DEPTH = NZ * SLOT


def split2(a):
    hi = a.astype(bf16)
    return hi, (a - hi.astype(f32)).astype(bf16)


def dot3(ah, al, bh, bl):
    d = functools.partial(jnp.dot, preferred_element_type=f32)
    return d(ah, bh) + (d(ah, bl) + d(al, bh))


WINDOWS = [(480 * t // 128 * 128, -(-480 * (t + 1) // 128) * 128) for t in range(4)]


def sort_columns(s_any, out_any, s_ref, out_ref, in_sems, out_sems):
    loads = [
        pltpu.make_async_copy(
            s_any.at[:, pl.ds(begin, end - begin)], s_ref.at[t, :, pl.ds(0, end - begin)], in_sems.at[t]
        )
        for t, (begin, end) in enumerate(WINDOWS)
    ]
    stores = [
        pltpu.make_async_copy(
            out_ref.at[:, :, pl.ds(128 * t, 128)], out_any.at[:, :, pl.ds(128 * t, 128)], out_sems.at[t]
        )
        for t in range(4)
    ]
    for load in loads:
        load.start()
    for t, (begin, end) in enumerate(WINDOWS):
        row = lax.broadcasted_iota(jnp.int32, (end - begin, 512), 0)
        col = lax.broadcasted_iota(jnp.int32, (end - begin, 512), 1)
        part, place = col // 128, col % 128
        zz, i = place // SLOT, place % SLOT
        target = 480 * t - begin + 120 * zz + SHARD * part + i
        pick = jnp.where((row == target) & (i < SHARD), 1.0, 0.0).astype(bf16)
        loads[t].wait()
        hi, lo = split2(s_ref[t, :, :end - begin])
        got = jnp.dot(hi, pick, preferred_element_type=f32) + jnp.dot(
            lo, pick, preferred_element_type=f32
        )
        for q in range(NY):
            for k in range(8):
                out_ref[q, SLOT * k:SLOT * k + SHARD, 128 * t:128 * t + 128] = got[
                    SHARD * k:SHARD * (k + 1), 128 * q:128 * q + 128
                ]
                out_ref[q, SLOT * k + SHARD:SLOT * (k + 1), 128 * t:128 * t + 128] = jnp.zeros(
                    (SLOT - SHARD, 128), f32
                )
        stores[t].start()
    for store in stores:
        store.wait()


def spread_columns(s):
    anywhere = pl.BlockSpec(memory_space=pltpu.HBM)
    return pl.pallas_call(
        sort_columns,
        out_shape=jax.ShapeDtypeStruct((NY, PAD, DEPTH), f32),
        in_specs=[anywhere],
        out_specs=anywhere,
        scratch_shapes=[
            pltpu.VMEM((4, ROWS, 640), f32),
            pltpu.VMEM((NY, PAD, DEPTH), f32),
            pltpu.SemaphoreType.DMA((4,)),
            pltpu.SemaphoreType.DMA((4,)),
        ],
        compiler_params=pltpu.CompilerParams(vmem_limit_bytes=8 << 20),
        cost_estimate=pl.CostEstimate(
            flops=2 * 2 * ROWS * 640 * 512 * 4, bytes_accessed=4 * 2 * ROWS * 2048, transcendentals=0
        ),
    )(s)


PIECES = ((-4, 0, 4), (-5, -1, 3), (-3, 1, 5), (8,), (-6, -2), (2, 6), (7,), (9,))
N_PIECES = len(PIECES)


def panel_kernel(where_ref, *refs):
    pieces, (pinv_ref, yh_ref, yl_ref, first_ref, second_ref, fac_ref) = refs[:N_PIECES], refs[N_PIECES:]
    z = where_ref[0]
    for ref, offsets in zip(pieces, PIECES):
        for k, offset in enumerate(offsets):
            slot = lax.rem(z + (offset + NZ), NZ)
            fac_ref[pl.ds(pl.multiple_of(slot * SLOT, SLOT), SLOT), :] = ref[SLOT * k:SLOT * (k + 1), :]
    for child in range(2):
        fh, fl = split2(fac_ref[:, C * child:C * (child + 1)])
        for j in range(2):
            ph, plo = split2(pinv_ref[child, :, 256 * j:256 * (j + 1)])
            yh, yl = split2(dot3(fh, fl, ph, plo))
            begin = C * child + 256 * j
            yh_ref[:, begin:begin + 256] = yh
            yl_ref[:, begin:begin + 256] = yl
    for k, out_ref in enumerate((first_ref, second_ref)):
        half = pl.ds(pl.multiple_of(lax.rem(z, 2) * PAD + HALF * k, HALF), HALF)
        out_ref[...] = yh_ref[half, :].astype(f32) + yl_ref[half, :].astype(f32)


def panel_rows(where, pieces, pinv):
    vmem = pl.BlockSpec(memory_space=pltpu.VMEM)
    split = jax.ShapeDtypeStruct((DEPTH, WIDE), bf16)
    return pl.pallas_call(
        panel_kernel,
        out_shape=(split, split) + (jax.ShapeDtypeStruct((HALF, WIDE), f32),) * 2,
        in_specs=[pl.BlockSpec(memory_space=pltpu.SMEM)] + [vmem] * (N_PIECES + 1),
        out_specs=(vmem,) * 4,
        scratch_shapes=[pltpu.VMEM((DEPTH, WIDE), f32)],
        compiler_params=pltpu.CompilerParams(vmem_limit_bytes=12 << 20),
        cost_estimate=pl.CostEstimate(
            flops=6 * 6 * DEPTH * WIDE * C, bytes_accessed=7 << 20, transcendentals=0
        ),
    )(where, *pieces, pinv)


def image_kernel(side, where_ref, yh_ref, yl_ref, s_ref, *refs):
    (*added_refs, out_ref, sh_ref, sl_ref) = refs
    half = where_ref[1] if side == 0 else 1 - where_ref[1]
    rows = pl.ds(pl.multiple_of(HALF * half, HALF), HALF)
    sh, sl = split2(jnp.concatenate([s_ref[k, rows, :] for k in range(NY)], axis=0))
    sh_ref[...] = sh
    sl_ref[...] = sl

    @pl.loop(0, WIDE // 256)
    def _(j):
        cols = pl.ds(pl.multiple_of(256 * j, 256), 256)
        u = dot3(sh_ref[...], sl_ref[...], yh_ref[:, cols], yl_ref[:, cols])
        for source in range(NY):
            for k in range(NY):
                begin = HALF * source + SLOT * k
                for g in range(2):
                    part = u[begin:begin + SLOT, OWN * g:OWN * (g + 1)]
                    at = (2 * j + g, k, slice(SLOT * source, SLOT * (source + 1)))
                    for ref in added_refs:
                        part = part + ref[at]
                    out_ref[at] = part


def partial_image(side, where, yh, yl, s_parts, *added):
    vmem = pl.BlockSpec(memory_space=pltpu.VMEM)
    return pl.pallas_call(
        functools.partial(image_kernel, side),
        out_shape=jax.ShapeDtypeStruct((NG, NY, HALF, OWN), f32),
        in_specs=[pl.BlockSpec(memory_space=pltpu.SMEM)] + [vmem] * (3 + len(added)),
        out_specs=vmem,
        scratch_shapes=[pltpu.VMEM((NY * HALF, DEPTH), bf16), pltpu.VMEM((NY * HALF, DEPTH), bf16)],
        compiler_params=pltpu.CompilerParams(vmem_limit_bytes=12 << 20),
        cost_estimate=pl.CostEstimate(
            flops=6 * DEPTH * WIDE * NY * HALF, bytes_accessed=6 << 20, transcendentals=0
        ),
    )(where, yh, yl, s_parts, *added)


def finish_kernel(block_ref, got_ref, weight_ref, y_ref, pivot_ref, off_ref, term_ref):
    halves = []
    for core in range(2):
        total = got_ref[0, core, 0]
        for x in range(4):
            for y in range(NY):
                if x or y:
                    total = total + got_ref[x, core, y]
        halves.append(total)
    rows = [halves[core][SLOT * y:SLOT * (y + 1)] for y in range(NY) for core in range(2)]
    z_own = weight_ref[...] * jnp.concatenate(rows, axis=0)
    off_ref[...] = -z_own
    zh, zl = split2(z_own)
    yh, yl = split2(y_ref[...].T)
    term_ref[...] = dot3(yh, yl, zh, zl)
    mine = pl.ds(pl.multiple_of(32 * block_ref[0], 32), 32)
    term_ref[mine, :] += pivot_ref[...]


def finish(block, got, weight, y_rows, pivot):
    return pl.pallas_call(
        finish_kernel,
        out_shape=(
            jax.ShapeDtypeStruct((PAD, OWN), f32),
            jax.ShapeDtypeStruct((C, OWN), f32),
        ),
        in_specs=[pl.BlockSpec(memory_space=pltpu.SMEM)] + [pl.BlockSpec(memory_space=pltpu.VMEM)] * 4,
        compiler_params=pltpu.CompilerParams(vmem_limit_bytes=10 << 20),
        cost_estimate=pl.CostEstimate(
            flops=6 * C * PAD * OWN, bytes_accessed=4 << 20, transcendentals=0
        ),
    )(block, got, weight, y_rows, pivot)


def pivot_solve(inverse, pivot_kind, pivot_diag, pivot_couple):
    diag_next = jnp.roll(pivot_diag, -1)
    diag_prev = jnp.roll(pivot_diag, 1)
    couple_prev = jnp.roll(pivot_couple, 1)
    det_here = pivot_diag * diag_next - pivot_couple * pivot_couple
    det_prev = diag_prev * pivot_diag - couple_prev * couple_prev
    self_coef = jnp.where(
        pivot_kind == 0,
        1.0 / pivot_diag,
        jnp.where(pivot_kind == 1, diag_next / det_here, diag_prev / det_prev),
    )
    next_coef = jnp.where(pivot_kind == 1, -pivot_couple / det_here, 0.0)
    prev_coef = jnp.where(pivot_kind == 2, -couple_prev / det_prev, 0.0)
    inv_next = jnp.roll(inverse, -1, axis=0)
    inv_prev = jnp.roll(inverse, 1, axis=0)
    return (
        self_coef[:, None] * inverse + next_coef[:, None] * inv_next + prev_coef[:, None] * inv_prev
    )


def shift_z(a, step):
    return lax.ppermute(a, Z, [(i, (i + step) % NZ) for i in range(NZ)])


def swap_core(a):
    return lax.ppermute(a, "c", [(0, 1), (1, 0)])


def place(x, core, z, y):
    return ((x * 2 + core) * NZ + z) * NY + y


def from_root_core(a):
    pairs = [
        (place(z // 4, z // 2 % 2, z, y), place(z // 4, 1 - z // 2 % 2, z, y)) for z in range(NZ) for y in range(NY)
    ]
    return lax.ppermute(a, AXES, pairs)


def from_root(a, step):
    pairs = [
        (place(z // 4, core, z, y), place((z // 4 + step) % 4, core, z, y))
        for z in range(NZ)
        for y in range(NY)
        for core in range(2)
    ]
    return lax.ppermute(a, AXES, pairs)


def exchange(a, axes):
    return lax.all_to_all(a, axes, 0, 0, tiled=True)


def per_device(s_parent, child_factor, panel_inverse, pivot_kind, pivot_diag, pivot_couple, child_mask):
    group = lax.axis_index(GRP)
    z = lax.axis_index(Z)
    y = lax.axis_index("y")
    core = lax.axis_index("c")
    branch = group // 4
    grid = z * NY + y
    flat = group * (NZ * NY) + grid

    weight = lax.dynamic_slice_in_dim(child_mask, flat * SHARD, SHARD, 1).astype(f32)
    weight = jnp.repeat(weight.T, C, axis=1)
    own = jnp.pad(weight * child_factor, ((0, SLOT - SHARD), (0, 0)))

    below, above = shift_z(own, 4), shift_z(own, -4)

    s_sorted = spread_columns(s_parent)
    s_parts = exchange(s_sorted, "y")
    near = jnp.concatenate([below, own, above], axis=0)
    low, high = shift_z(near, 1), shift_z(near, -1)
    far = shift_z(below, 4)
    low2, high2 = shift_z(low[0:64], 1), shift_z(high[32:96], -1)
    low_far, high_far = shift_z(far, 1), shift_z(far, -1)
    pieces = (near, low, high, far, low2, high2, low_far, high_far)

    inverse = lax.dynamic_index_in_dim(panel_inverse, branch, 0, keepdims=False)

    inverse_cols = lax.dynamic_slice_in_dim(inverse, group % 4 * OWN, OWN, 1)
    kinds = lax.dynamic_index_in_dim(pivot_kind, branch, 0, keepdims=False)
    diags = lax.dynamic_index_in_dim(pivot_diag, branch, 0, keepdims=False)
    couples = lax.dynamic_index_in_dim(pivot_couple, branch, 0, keepdims=False)
    scaled = pivot_solve(inverse_cols, kinds, diags, couples)
    block = z % 4 * NY + y
    pivot_part = lax.dot_general(
        lax.dynamic_slice_in_dim(inverse, block * 32, 32, 1),
        scaled,
        (((0,), (0,)), ((), ())),
        precision=highest,
        preferred_element_type=f32,
    )
    pivot_part = jnp.where(lax.axis_index("h") == 0, pivot_part, 0.0)
    tile_weight = lax.dynamic_slice(child_mask, (branch, NY * ROWS * z), (1, NY * ROWS)).astype(f32)
    tile_weight = lax.dynamic_index_in_dim(tile_weight.reshape(NY, 2, NY, SHARD), y, 2, keepdims=False)
    tile_weight = jnp.pad(tile_weight, ((0, 0), (0, 0), (0, SLOT - SHARD))).reshape(PAD, 1)

    where = jnp.stack([z, core]).astype(jnp.int32)
    yh, yl, first, second = panel_rows(where, pieces, panel_inverse)
    at_core = core == z // 2 % 2
    half = jnp.where(at_core, first, from_root_core(second))
    send = partial_image(1, where, yh, yl, s_parts)
    received = swap_core(send)
    half, yh, yl = lax.optimization_barrier((half, yh, yl))
    x = lax.axis_index("x")
    parts = [
        from_root(lax.dynamic_slice_in_dim(half, (x + step) % 4 // 2 * C, C, 1), step) for step in (2, 1, 3)
    ]
    image = partial_image(0, where, yh, yl, s_parts, received)
    image, *parts = lax.optimization_barrier((image, *parts))
    got = exchange(image.reshape(32 * HALF, OWN), PLANE)
    kept = lax.dynamic_slice_in_dim(half, x // 2 * C, C, 1)
    mine = jnp.where(x == z // 4, kept, parts[0] + parts[1] + parts[2])
    other = swap_core(mine)
    y_rows = jnp.concatenate([jnp.where(at_core, mine, other), jnp.where(at_core, other, mine)], axis=0)

    off, term = finish(
        block.reshape(1).astype(jnp.int32), got.reshape(4, 2, NY, HALF, OWN), tile_weight, y_rows, pivot_part
    )

    rows = exchange(term, ("l", "y")).reshape(16, 32, OWN).sum(0)
    blocks = [
        lax.ppermute(
            lax.dynamic_slice_in_dim(off, (y + step) % NY * 2 * SLOT, 2 * SLOT, 0),
            "y", [(i, (i + step) % NY) for i in range(NY)],
        ) if step else lax.dynamic_slice_in_dim(off, y * 2 * SLOT, 2 * SLOT, 0)
        for step in range(NY)
    ]
    rows = exchange(jnp.tile(rows, (4, 1)), "h").reshape(4, 32, OWN).sum(0)
    panel = exchange(jnp.tile(rows, (16, 1)), ("l", "y"))
    blocks = jnp.stack([b.reshape(2, SLOT, OWN)[:, :SHARD] for b in blocks[::-1] + blocks[:0:-1]])
    off = lax.dynamic_slice_in_dim(blocks, 3 - y, NY, 0).transpose(1, 0, 2, 3).reshape(ROWS, OWN)
    return off, panel


def solution(mesh):
    grid = Mesh(mesh.devices.reshape(4, 2, 4, 4, 4), AXES)
    lines = ("h", "l", "y")
    placed = (P(lines, GRP), P(AXES, None), P(), P(), P(), P(), P())
    return jax.shard_map(
        per_device,
        mesh=grid,
        in_specs=placed,
        out_specs=(P(lines, GRP), P(None, GRP)),
        check_vma=False,
    )
```

```python
import functools

import jax
import jax.numpy as jnp
import numpy as np
from jax import lax
from jax.experimental import pallas as pl
from jax.experimental.pallas import tpu as pltpu
from jax.sharding import Mesh
from jax.sharding import PartitionSpec as P

f32, bf16 = jnp.float32, jnp.bfloat16
highest = lax.Precision.HIGHEST

AXES = ("x", "c", "h", "l", "y")
Z = ("h", "l")
GRP = ("x", "c")
PLANE = ("x", "c", "y")
NZ, NY, NG = 16, 4, 8
SHARD = 30
SLOT = 32
ROWS = 240
PAD = 256
HALF = PAD // 2
COLS = 1920
WIDE = 1024
C = 512
OWN = 128
DEPTH = NZ * SLOT


def split2(a):
    hi = a.astype(bf16)
    return hi, (a - hi.astype(f32)).astype(bf16)


def dot3(ah, al, bh, bl):
    d = functools.partial(jnp.dot, preferred_element_type=f32)
    return d(ah, bh) + (d(ah, bl) + d(al, bh))


WINDOWS = [(480 * t // 128 * 128, -(-480 * (t + 1) // 128) * 128) for t in range(4)]


def sort_columns(s_any, out_any, s_ref, out_ref, in_sems, out_sems):
    loads = [
        pltpu.make_async_copy(
            s_any.at[:, pl.ds(begin, end - begin)], s_ref.at[t, :, pl.ds(0, end - begin)], in_sems.at[t]
        )
        for t, (begin, end) in enumerate(WINDOWS)
    ]
    stores = [
        pltpu.make_async_copy(
            out_ref.at[:, :, pl.ds(128 * t, 128)], out_any.at[:, :, pl.ds(128 * t, 128)], out_sems.at[t]
        )
        for t in range(4)
    ]
    for load in loads:
        load.start()
    for t, (begin, end) in enumerate(WINDOWS):
        row = lax.broadcasted_iota(jnp.int32, (end - begin, 512), 0)
        col = lax.broadcasted_iota(jnp.int32, (end - begin, 512), 1)
        part, place = col // 128, col % 128
        zz, i = place // SLOT, place % SLOT
        target = 480 * t - begin + 120 * zz + SHARD * part + i
        pick = jnp.where((row == target) & (i < SHARD), 1.0, 0.0).astype(bf16)
        loads[t].wait()
        hi, lo = split2(s_ref[t, :, :end - begin])
        got = jnp.dot(hi, pick, preferred_element_type=f32) + jnp.dot(
            lo, pick, preferred_element_type=f32
        )
        for q in range(NY):
            for k in range(8):
                out_ref[q, SLOT * k:SLOT * k + SHARD, 128 * t:128 * t + 128] = got[
                    SHARD * k:SHARD * (k + 1), 128 * q:128 * q + 128
                ]
                out_ref[q, SLOT * k + SHARD:SLOT * (k + 1), 128 * t:128 * t + 128] = jnp.zeros(
                    (SLOT - SHARD, 128), f32
                )
        stores[t].start()
    for store in stores:
        store.wait()


def spread_columns(s):
    anywhere = pl.BlockSpec(memory_space=pltpu.HBM)
    return pl.pallas_call(
        sort_columns,
        out_shape=jax.ShapeDtypeStruct((NY, PAD, DEPTH), f32),
        in_specs=[anywhere],
        out_specs=anywhere,
        scratch_shapes=[
            pltpu.VMEM((4, ROWS, 640), f32),
            pltpu.VMEM((NY, PAD, DEPTH), f32),
            pltpu.SemaphoreType.DMA((4,)),
            pltpu.SemaphoreType.DMA((4,)),
        ],
        compiler_params=pltpu.CompilerParams(vmem_limit_bytes=8 << 20),
        cost_estimate=pl.CostEstimate(
            flops=2 * 2 * ROWS * 640 * 512 * 4, bytes_accessed=4 * 2 * ROWS * 2048, transcendentals=0
        ),
    )(s)


PIECES = ((-4, 0, 4), (-5, -1, 3), (-3, 1, 5), (8,), (-6, -2), (2, 6), (7,), (9,))
N_PIECES = len(PIECES)


def image_rows(half, yh_ref, yl_ref, s_ref, out_ref, sh_ref, sl_ref, added_ref=None):
    rows = pl.ds(pl.multiple_of(HALF * half, HALF), HALF)
    sh, sl = split2(jnp.concatenate([s_ref[k, rows, :] for k in range(NY)], axis=0))
    sh_ref[...] = sh
    sl_ref[...] = sl

    @pl.loop(0, WIDE // 256)
    def _(j):
        cols = pl.ds(pl.multiple_of(256 * j, 256), 256)
        u = dot3(sh_ref[...], sl_ref[...], yh_ref[:, cols], yl_ref[:, cols])
        for source in range(NY):
            for k in range(NY):
                begin = HALF * source + SLOT * k
                for g in range(2):
                    part = u[begin:begin + SLOT, OWN * g:OWN * (g + 1)]
                    at = (2 * j + g, k, slice(SLOT * source, SLOT * (source + 1)))
                    out_ref[at] = part if added_ref is None else part + added_ref[at]


def panel_kernel(where_ref, *refs):
    pieces, (pinv_ref, yh_ref, yl_ref, fac_ref) = refs[:N_PIECES], refs[N_PIECES:]
    z = where_ref[0]
    for ref, offsets in zip(pieces, PIECES):
        for k, offset in enumerate(offsets):
            slot = lax.rem(z + (1 - 2 * where_ref[1]) * offset + NZ, NZ)
            fac_ref[pl.ds(pl.multiple_of(slot * SLOT, SLOT), SLOT), :] = ref[SLOT * k:SLOT * (k + 1), :]
    for child in range(2):
        fh, fl = split2(fac_ref[:, C * child:C * (child + 1)])
        for j in range(2):
            ph, plo = split2(pinv_ref[child, :, 256 * j:256 * (j + 1)])
            yh, yl = split2(dot3(fh, fl, ph, plo))
            begin = C * child + 256 * j
            yh_ref[:, begin:begin + 256] = yh
            yl_ref[:, begin:begin + 256] = yl


def panel_rows(where, pieces, pinv):
    vmem = pl.BlockSpec(memory_space=pltpu.VMEM)
    split = jax.ShapeDtypeStruct((DEPTH, WIDE), bf16)
    return pl.pallas_call(
        panel_kernel,
        out_shape=(split, split),
        in_specs=[pl.BlockSpec(memory_space=pltpu.SMEM)] + [vmem] * (N_PIECES + 1),
        out_specs=(vmem, vmem),
        scratch_shapes=[pltpu.VMEM((DEPTH, WIDE), f32)],
        compiler_params=pltpu.CompilerParams(vmem_limit_bytes=12 << 20),
        cost_estimate=pl.CostEstimate(
            flops=6 * 6 * DEPTH * WIDE * C, bytes_accessed=7 << 20, transcendentals=0
        ),
    )(where, *pieces, pinv)


STEPS = (0, 2, 1, 3)


def other_kernel(where_ref, yh_ref, yl_ref, s_ref, send_ref, *refs):
    *own_refs, sh_ref, sl_ref = refs
    rows = pl.ds(pl.multiple_of(lax.rem(where_ref[0], 2) * PAD, PAD), PAD)
    for step, out_ref in zip(STEPS, own_refs):
        child = lax.rem(where_ref[2] + step, 4) // 2
        cols = pl.ds(pl.multiple_of(child * C, C), C)
        out_ref[...] = yh_ref[rows, cols].astype(f32) + yl_ref[rows, cols].astype(f32)
    image_rows(1 - where_ref[1], yh_ref, yl_ref, s_ref, send_ref, sh_ref, sl_ref)


def other_image(where, yh, yl, s_parts):
    vmem = pl.BlockSpec(memory_space=pltpu.VMEM)
    own = jax.ShapeDtypeStruct((PAD, C), f32)
    return pl.pallas_call(
        other_kernel,
        out_shape=(jax.ShapeDtypeStruct((NG, NY, HALF, OWN), f32),) + (own,) * 4,
        in_specs=[pl.BlockSpec(memory_space=pltpu.SMEM)] + [vmem] * 3,
        out_specs=(vmem,) * 5,
        scratch_shapes=[pltpu.VMEM((NY * HALF, DEPTH), bf16), pltpu.VMEM((NY * HALF, DEPTH), bf16)],
        compiler_params=pltpu.CompilerParams(vmem_limit_bytes=14 << 20),
        cost_estimate=pl.CostEstimate(
            flops=6 * DEPTH * WIDE * NY * HALF, bytes_accessed=8 << 20, transcendentals=0
        ),
    )(where, yh, yl, s_parts)


def image_kernel(where_ref, yh_ref, yl_ref, s_ref, added_ref, out_ref, sh_ref, sl_ref):
    image_rows(where_ref[1], yh_ref, yl_ref, s_ref, out_ref, sh_ref, sl_ref, added_ref)


def own_image(where, yh, yl, s_parts, added):
    vmem = pl.BlockSpec(memory_space=pltpu.VMEM)
    return pl.pallas_call(
        image_kernel,
        out_shape=jax.ShapeDtypeStruct((NG, NY, HALF, OWN), f32),
        in_specs=[pl.BlockSpec(memory_space=pltpu.SMEM)] + [vmem] * 4,
        out_specs=vmem,
        scratch_shapes=[pltpu.VMEM((NY * HALF, DEPTH), bf16), pltpu.VMEM((NY * HALF, DEPTH), bf16)],
        compiler_params=pltpu.CompilerParams(vmem_limit_bytes=14 << 20),
        cost_estimate=pl.CostEstimate(
            flops=6 * DEPTH * WIDE * NY * HALF, bytes_accessed=6 << 20, transcendentals=0
        ),
    )(where, yh, yl, s_parts, added)


def finish_kernel(block_ref, got_ref, weight_ref, y_ref, pivot_ref, off_ref, term_ref):
    halves = []
    for core in range(2):
        total = got_ref[0, core, 0]
        for x in range(4):
            for y in range(NY):
                if x or y:
                    total = total + got_ref[x, core, y]
        halves.append(total)
    rows = [halves[core][SLOT * y:SLOT * (y + 1)] for y in range(NY) for core in range(2)]
    z_own = weight_ref[...] * jnp.concatenate(rows, axis=0)
    off_ref[...] = -z_own
    zh, zl = split2(z_own)
    yh, yl = split2(y_ref[...].T)
    term_ref[...] = dot3(yh, yl, zh, zl)
    mine = pl.ds(pl.multiple_of(32 * block_ref[0], 32), 32)
    term_ref[mine, :] += pivot_ref[...]


def finish(block, got, weight, y_rows, pivot):
    return pl.pallas_call(
        finish_kernel,
        out_shape=(
            jax.ShapeDtypeStruct((PAD, OWN), f32),
            jax.ShapeDtypeStruct((C, OWN), f32),
        ),
        in_specs=[pl.BlockSpec(memory_space=pltpu.SMEM)] + [pl.BlockSpec(memory_space=pltpu.VMEM)] * 4,
        compiler_params=pltpu.CompilerParams(vmem_limit_bytes=10 << 20),
        cost_estimate=pl.CostEstimate(
            flops=6 * C * PAD * OWN, bytes_accessed=4 << 20, transcendentals=0
        ),
    )(block, got, weight, y_rows, pivot)


def pivot_solve(inverse, pivot_kind, pivot_diag, pivot_couple):
    diag_next = jnp.roll(pivot_diag, -1)
    diag_prev = jnp.roll(pivot_diag, 1)
    couple_prev = jnp.roll(pivot_couple, 1)
    det_here = pivot_diag * diag_next - pivot_couple * pivot_couple
    det_prev = diag_prev * pivot_diag - couple_prev * couple_prev
    self_coef = jnp.where(
        pivot_kind == 0,
        1.0 / pivot_diag,
        jnp.where(pivot_kind == 1, diag_next / det_here, diag_prev / det_prev),
    )
    next_coef = jnp.where(pivot_kind == 1, -pivot_couple / det_here, 0.0)
    prev_coef = jnp.where(pivot_kind == 2, -couple_prev / det_prev, 0.0)
    inv_next = jnp.roll(inverse, -1, axis=0)
    inv_prev = jnp.roll(inverse, 1, axis=0)
    return (
        self_coef[:, None] * inverse + next_coef[:, None] * inv_next + prev_coef[:, None] * inv_prev
    )


def shift_z(a, step):
    pairs = [
        (core * NZ + z, core * NZ + (z + (1 - 2 * core) * step) % NZ) for core in range(2) for z in range(NZ)
    ]
    return lax.ppermute(a, ("c",) + Z, pairs)


def swap_core(a):
    return lax.ppermute(a, "c", [(0, 1), (1, 0)])


def place(x, core, z, y):
    return ((x * 2 + core) * NZ + z) * NY + y


def to_other_core(a):
    pairs = [
        (place(x, z // 2 % 2, z, y), place(x, 1 - z // 2 % 2, z, y))
        for x in range(4)
        for z in range(NZ)
        for y in range(NY)
    ]
    return lax.ppermute(a, AXES, pairs)


def from_root(a, step):
    pairs = [
        (place(z // 4, z // 2 % 2, z, y), place((z // 4 + step) % 4, z // 2 % 2, z, y))
        for z in range(NZ)
        for y in range(NY)
    ]
    return lax.ppermute(a, AXES, pairs)


def block_for(off, y):
    return lax.dynamic_slice_in_dim(off, y * 2 * SLOT, 2 * SLOT, 0)


def swap_y(a, bit):
    return lax.ppermute(a, "y", [(i, i ^ bit) for i in range(NY)])


def order_kernel(y_ref, off_ref, first_ref, second_ref, out_ref):
    y = y_ref[0]
    block = 2 * SLOT
    own = off_ref[pl.ds(pl.multiple_of(block * y, block), block), :]
    got = own, first_ref[:block], second_ref[:block], second_ref[block:]
    for source in range(NY):
        at = source ^ y
        rows = jnp.where(at == 0, got[0], jnp.where(at == 1, got[1], jnp.where(at == 2, got[2], got[3])))
        for k in range(2):
            begin = 120 * k + SHARD * source
            out_ref[begin:begin + SHARD, :] = rows[SLOT * k:SLOT * k + SHARD]


def in_order(y, off, first, second):
    vmem = pl.BlockSpec(memory_space=pltpu.VMEM)
    return pl.pallas_call(
        order_kernel,
        out_shape=jax.ShapeDtypeStruct((ROWS, OWN), f32),
        in_specs=[pl.BlockSpec(memory_space=pltpu.SMEM)] + [vmem] * 3,
        out_specs=vmem,
    )(y, off, first, second)


def exchange(a, axes):
    return lax.all_to_all(a, axes, 0, 0, tiled=True)


def per_device(s_parent, child_factor, panel_inverse, pivot_kind, pivot_diag, pivot_couple, child_mask):
    group = lax.axis_index(GRP)
    z = lax.axis_index(Z)
    y = lax.axis_index("y")
    core = lax.axis_index("c")
    branch = group // 4
    grid = z * NY + y
    flat = group * (NZ * NY) + grid

    weight = lax.dynamic_slice_in_dim(child_mask, flat * SHARD, SHARD, 1).astype(f32)
    weight = jnp.repeat(weight.T, C, axis=1)
    own = jnp.pad(weight * child_factor, ((0, SLOT - SHARD), (0, 0)))

    below, above = shift_z(own, 4), shift_z(own, -4)

    s_sorted = spread_columns(s_parent)
    s_parts = exchange(s_sorted, "y")
    near = jnp.concatenate([below, own, above], axis=0)
    low, high = shift_z(near, 1), shift_z(near, -1)
    far = shift_z(below, 4)
    low2, high2 = shift_z(low[0:64], 1), shift_z(high[32:96], -1)
    low_far, high_far = shift_z(far, 1), shift_z(far, -1)
    pieces = (near, low, high, far, low2, high2, low_far, high_far)

    inverse = lax.dynamic_index_in_dim(panel_inverse, branch, 0, keepdims=False)

    inverse_cols = lax.dynamic_slice_in_dim(inverse, group % 4 * OWN, OWN, 1)
    kinds = lax.dynamic_index_in_dim(pivot_kind, branch, 0, keepdims=False)
    diags = lax.dynamic_index_in_dim(pivot_diag, branch, 0, keepdims=False)
    couples = lax.dynamic_index_in_dim(pivot_couple, branch, 0, keepdims=False)
    scaled = pivot_solve(inverse_cols, kinds, diags, couples)
    block = z % 4 * NY + y
    pivot_part = lax.dot_general(
        lax.dynamic_slice_in_dim(inverse, block * 32, 32, 1),
        scaled,
        (((0,), (0,)), ((), ())),
        precision=highest,
        preferred_element_type=f32,
    )
    pivot_part = jnp.where(lax.axis_index("h") == 0, pivot_part, 0.0)
    tile_weight = lax.dynamic_slice(child_mask, (branch, NY * ROWS * z), (1, NY * ROWS)).astype(f32)
    tile_weight = lax.dynamic_index_in_dim(tile_weight.reshape(NY, 2, NY, SHARD), y, 2, keepdims=False)
    tile_weight = jnp.pad(tile_weight, ((0, 0), (0, 0), (0, SLOT - SHARD))).reshape(PAD, 1)

    x = lax.axis_index("x")
    where = jnp.stack([z, core, x]).astype(jnp.int32)
    yh, yl = panel_rows(where, pieces, panel_inverse)
    send, kept, *leaving = other_image(where, yh, yl, s_parts)

    parts = [from_root(a, step) for a, step in zip(leaving, STEPS[1:])]
    image = own_image(where, yh, yl, s_parts, swap_core(send))
    image, *parts = lax.optimization_barrier((image, *parts))
    got = exchange(image.reshape(32 * HALF, OWN), PLANE)
    mine = jnp.where(x == z // 4, kept, parts[0] + parts[1] + parts[2])
    y_rows = jnp.where(core == z // 2 % 2, mine, to_other_core(mine))

    off, term = finish(
        block.reshape(1).astype(jnp.int32), got.reshape(4, 2, NY, HALF, OWN), tile_weight, y_rows, pivot_part
    )

    rows = exchange(term, ("l", "y")).reshape(16, 32, OWN).sum(0)
    first = swap_y(jnp.concatenate([block_for(off, y ^ 1), block_for(off, y ^ 3)], axis=0), 1)
    rows, first = lax.optimization_barrier((rows, first))
    second = swap_y(jnp.concatenate([block_for(off, y ^ 2), first[2 * SLOT:]], axis=0), 2)
    rows = exchange(jnp.tile(rows, (4, 1)), "h").reshape(4, 32, OWN).sum(0)
    panel = exchange(jnp.tile(rows, (16, 1)), ("l", "y"))
    off = in_order(y.reshape(1).astype(jnp.int32), off, first, second)
    return off, panel


def solution(mesh):
    grid = Mesh(mesh.devices.reshape(4, 2, 4, 4, 4), AXES)
    lines = ("h", "l", "y")
    placed = (P(lines, GRP), P(AXES, None), P(), P(), P(), P(), P())
    return jax.shard_map(
        per_device,
        mesh=grid,
        in_specs=placed,
        out_specs=(P(lines, GRP), P(None, GRP)),
        check_vma=False,
    )
```

```python
import functools

import jax
import jax.numpy as jnp
import numpy as np
from jax import lax
from jax.experimental import pallas as pl
from jax.experimental.pallas import tpu as pltpu
from jax.sharding import Mesh
from jax.sharding import PartitionSpec as P

f32, bf16 = jnp.float32, jnp.bfloat16
highest = lax.Precision.HIGHEST

AXES = ("x", "c", "h", "l", "y")
Z = ("h", "l")
GRP = ("x", "c")
PLANE = ("x", "c", "y")
NZ, NY, NG = 16, 4, 8
SHARD = 30
SLOT = 32
ROWS = 240
PAD = 256
HALF = PAD // 2
COLS = 1920
WIDE = 1024
C = 512
OWN = 128
DEPTH = NZ * SLOT


def split2(a):
    hi = a.astype(bf16)
    return hi, (a - hi.astype(f32)).astype(bf16)


def dot3(ah, al, bh, bl):
    d = functools.partial(jnp.dot, preferred_element_type=f32)
    return d(ah, bh) + (d(ah, bl) + d(al, bh))


WINDOWS = [(480 * t // 128 * 128, -(-480 * (t + 1) // 128) * 128) for t in range(4)]


def sort_columns(s_any, out_any, s_ref, out_ref, in_sems, out_sems):
    loads = [
        pltpu.make_async_copy(
            s_any.at[:, pl.ds(begin, end - begin)], s_ref.at[t, :, pl.ds(0, end - begin)], in_sems.at[t]
        )
        for t, (begin, end) in enumerate(WINDOWS)
    ]
    stores = [
        pltpu.make_async_copy(
            out_ref.at[:, :, pl.ds(128 * t, 128)], out_any.at[:, :, pl.ds(128 * t, 128)], out_sems.at[t]
        )
        for t in range(4)
    ]
    for load in loads:
        load.start()
    for t, (begin, end) in enumerate(WINDOWS):
        row = lax.broadcasted_iota(jnp.int32, (end - begin, 512), 0)
        col = lax.broadcasted_iota(jnp.int32, (end - begin, 512), 1)
        part, place = col // 128, col % 128
        zz, i = place // SLOT, place % SLOT
        target = 480 * t - begin + 120 * zz + SHARD * part + i
        pick = jnp.where((row == target) & (i < SHARD), 1.0, 0.0).astype(bf16)
        loads[t].wait()
        hi, lo = split2(s_ref[t, :, :end - begin])
        got = jnp.dot(hi, pick, preferred_element_type=f32) + jnp.dot(
            lo, pick, preferred_element_type=f32
        )
        for q in range(NY):
            for k in range(8):
                part, begin, cols = k // 4 * NY + q, SLOT * (k % 4), slice(128 * t, 128 * t + 128)
                out_ref[part, begin:begin + SHARD, cols] = got[
                    SHARD * k:SHARD * (k + 1), 128 * q:128 * q + 128
                ]
                out_ref[part, begin + SHARD:begin + SLOT, cols] = jnp.zeros((SLOT - SHARD, 128), f32)
        stores[t].start()
    for store in stores:
        store.wait()


def spread_columns(s):
    anywhere = pl.BlockSpec(memory_space=pltpu.HBM)
    return pl.pallas_call(
        sort_columns,
        out_shape=jax.ShapeDtypeStruct((2 * NY, HALF, DEPTH), f32),
        in_specs=[anywhere],
        out_specs=anywhere,
        scratch_shapes=[
            pltpu.VMEM((4, ROWS, 640), f32),
            pltpu.VMEM((2 * NY, HALF, DEPTH), f32),
            pltpu.SemaphoreType.DMA((4,)),
            pltpu.SemaphoreType.DMA((4,)),
        ],
        compiler_params=pltpu.CompilerParams(vmem_limit_bytes=8 << 20),
        cost_estimate=pl.CostEstimate(
            flops=2 * 2 * ROWS * 640 * 512 * 4, bytes_accessed=4 * 2 * ROWS * 2048, transcendentals=0
        ),
    )(s)


PIECES = ((-4, 0, 4), (-5, -1, 3), (-3, 1, 5), (8,), (-6, -2, 7), (2, 6, 9))
N_PIECES = len(PIECES)


STEPS = (0, 2, 1, 3)


def panel_kernel(where_ref, *refs):
    pieces, (pinv_ref, y_ref, *own_refs, fac_ref) = refs[:N_PIECES], refs[N_PIECES:]
    z, core, x = where_ref[0], where_ref[1], where_ref[2]
    for ref, offsets in zip(pieces, PIECES):
        for k, offset in enumerate(offsets):
            slot = lax.rem(z + (1 - 2 * core) * offset + NZ, NZ)
            fac_ref[pl.ds(pl.multiple_of(slot * SLOT, SLOT), SLOT), :] = ref[SLOT * k:SLOT * (k + 1), :]
    for child in range(2):
        fh, fl = split2(fac_ref[:, C * child:C * (child + 1)])
        for j in range(2):
            ph, plo = split2(pinv_ref[child, :, 256 * j:256 * (j + 1)])
            begin = C * child + 256 * j
            y_ref[:, begin:begin + 256] = dot3(fh, fl, ph, plo)
    rows = pl.ds(pl.multiple_of(lax.rem(z, 2) * PAD, PAD), PAD)
    for step, out_ref in zip(STEPS, own_refs):
        child = lax.rem(x + step, 4) // 2
        out_ref[...] = y_ref[rows, pl.ds(pl.multiple_of(child * C, C), C)]


def panel_rows(where, pieces, pinv):
    vmem = pl.BlockSpec(memory_space=pltpu.VMEM)
    own = jax.ShapeDtypeStruct((PAD, C), f32)
    return pl.pallas_call(
        panel_kernel,
        out_shape=(jax.ShapeDtypeStruct((DEPTH, WIDE), f32),) + (own,) * 4,
        in_specs=[pl.BlockSpec(memory_space=pltpu.SMEM)] + [vmem] * (N_PIECES + 1),
        out_specs=(vmem,) * 5,
        scratch_shapes=[pltpu.VMEM((DEPTH, WIDE), f32)],
        compiler_params=pltpu.CompilerParams(vmem_limit_bytes=14 << 20),
        cost_estimate=pl.CostEstimate(
            flops=5 * 6 * DEPTH * WIDE * C, bytes_accessed=9 << 20, transcendentals=0
        ),
    )(where, *pieces, pinv)


def image_kernel(where_ref, y_ref, other_ref, s_ref, out_ref, sh_ref, sl_ref):
    core = where_ref[1]
    for side in range(2):
        first = NY * (core if side == 0 else 1 - core)
        sh, sl = split2(jnp.concatenate([s_ref[first + k] for k in range(NY)], axis=0))
        sh_ref[side] = sh
        sl_ref[side] = sl

    @pl.loop(0, WIDE // 256)
    def _(j):
        cols = pl.ds(pl.multiple_of(256 * j, 256), 256)
        u = dot3(sh_ref[0], sl_ref[0], *split2(y_ref[:, cols]))
        u = u + dot3(sh_ref[1], sl_ref[1], *split2(other_ref[:, cols]))
        for source in range(NY):
            for k in range(NY):
                begin = HALF * source + SLOT * k
                for g in range(2):
                    out_ref[2 * j + g, k, SLOT * source:SLOT * (source + 1), :] = u[
                        begin:begin + SLOT, OWN * g:OWN * (g + 1)
                    ]


def chip_image(where, y_rows, other, s_parts):
    vmem = pl.BlockSpec(memory_space=pltpu.VMEM)
    return pl.pallas_call(
        image_kernel,
        out_shape=jax.ShapeDtypeStruct((NG, NY, HALF, OWN), f32),
        in_specs=[pl.BlockSpec(memory_space=pltpu.SMEM)] + [vmem] * 3,
        out_specs=vmem,
        scratch_shapes=[pltpu.VMEM((2, NY * HALF, DEPTH), bf16), pltpu.VMEM((2, NY * HALF, DEPTH), bf16)],
        compiler_params=pltpu.CompilerParams(vmem_limit_bytes=16 << 20),
        cost_estimate=pl.CostEstimate(
            flops=12 * DEPTH * WIDE * NY * HALF, bytes_accessed=8 << 20, transcendentals=0
        ),
    )(where, y_rows, other, s_parts)


def finish_kernel(block_ref, got_ref, weight_ref, y_ref, pivot_ref, off_ref, term_ref):
    halves = []
    for core in range(2):
        total = got_ref[0, core, 0]
        for x in range(4):
            for y in range(NY):
                if x or y:
                    total = total + got_ref[x, core, y]
        halves.append(total)
    rows = [halves[core][SLOT * y:SLOT * (y + 1)] for y in range(NY) for core in range(2)]
    z_own = weight_ref[...] * jnp.concatenate(rows, axis=0)
    off_ref[...] = -z_own
    zh, zl = split2(z_own)
    yh, yl = split2(y_ref[...].T)
    term_ref[...] = dot3(yh, yl, zh, zl)
    mine = pl.ds(pl.multiple_of(32 * block_ref[0], 32), 32)
    term_ref[mine, :] += pivot_ref[...]


def finish(block, got, weight, y_rows, pivot):
    return pl.pallas_call(
        finish_kernel,
        out_shape=(
            jax.ShapeDtypeStruct((PAD, OWN), f32),
            jax.ShapeDtypeStruct((C, OWN), f32),
        ),
        in_specs=[pl.BlockSpec(memory_space=pltpu.SMEM)] + [pl.BlockSpec(memory_space=pltpu.VMEM)] * 4,
        compiler_params=pltpu.CompilerParams(vmem_limit_bytes=10 << 20),
        cost_estimate=pl.CostEstimate(
            flops=6 * C * PAD * OWN, bytes_accessed=4 << 20, transcendentals=0
        ),
    )(block, got, weight, y_rows, pivot)


def pivot_solve(inverse, pivot_kind, pivot_diag, pivot_couple):
    diag_next = jnp.roll(pivot_diag, -1)
    diag_prev = jnp.roll(pivot_diag, 1)
    couple_prev = jnp.roll(pivot_couple, 1)
    det_here = pivot_diag * diag_next - pivot_couple * pivot_couple
    det_prev = diag_prev * pivot_diag - couple_prev * couple_prev
    self_coef = jnp.where(
        pivot_kind == 0,
        1.0 / pivot_diag,
        jnp.where(pivot_kind == 1, diag_next / det_here, diag_prev / det_prev),
    )
    next_coef = jnp.where(pivot_kind == 1, -pivot_couple / det_here, 0.0)
    prev_coef = jnp.where(pivot_kind == 2, -couple_prev / det_prev, 0.0)
    inv_next = jnp.roll(inverse, -1, axis=0)
    inv_prev = jnp.roll(inverse, 1, axis=0)
    return (
        self_coef[:, None] * inverse + next_coef[:, None] * inv_next + prev_coef[:, None] * inv_prev
    )


def shift_z(a, step):
    pairs = [
        (core * NZ + z, core * NZ + (z + (1 - 2 * core) * step) % NZ) for core in range(2) for z in range(NZ)
    ]
    return lax.ppermute(a, ("c",) + Z, pairs)


def swap_core(a):
    return lax.ppermute(a, "c", [(0, 1), (1, 0)])


def place(x, core, z, y):
    return ((x * 2 + core) * NZ + z) * NY + y


def to_other_core(a):
    pairs = [
        (place(x, z // 2 % 2, z, y), place(x, 1 - z // 2 % 2, z, y))
        for x in range(4)
        for z in range(NZ)
        for y in range(NY)
    ]
    return lax.ppermute(a, AXES, pairs)


def from_root(a, step):
    pairs = [
        (place(z // 4, z // 2 % 2, z, y), place((z // 4 + step) % 4, z // 2 % 2, z, y))
        for z in range(NZ)
        for y in range(NY)
    ]
    return lax.ppermute(a, AXES, pairs)


def block_for(off, y):
    return lax.dynamic_slice_in_dim(off, y * 2 * SLOT, 2 * SLOT, 0)


def swap_y(a, bit):
    return lax.ppermute(a, "y", [(i, i ^ bit) for i in range(NY)])


def order_kernel(y_ref, off_ref, first_ref, second_ref, out_ref):
    y = y_ref[0]
    block = 2 * SLOT
    own = off_ref[pl.ds(pl.multiple_of(block * y, block), block), :]
    got = own, second_ref[:block], first_ref[:block], second_ref[block:]
    for source in range(NY):
        at = source ^ y
        rows = jnp.where(at == 0, got[0], jnp.where(at == 1, got[1], jnp.where(at == 2, got[2], got[3])))
        for k in range(2):
            begin = 120 * k + SHARD * source
            out_ref[begin:begin + SHARD, :] = rows[SLOT * k:SLOT * k + SHARD]


def in_order(y, off, first, second):
    vmem = pl.BlockSpec(memory_space=pltpu.VMEM)
    return pl.pallas_call(
        order_kernel,
        out_shape=jax.ShapeDtypeStruct((ROWS, OWN), f32),
        in_specs=[pl.BlockSpec(memory_space=pltpu.SMEM)] + [vmem] * 3,
        out_specs=vmem,
    )(y, off, first, second)


def exchange(a, axes):
    return lax.all_to_all(a, axes, 0, 0, tiled=True)


def per_device(s_parent, child_factor, panel_inverse, pivot_kind, pivot_diag, pivot_couple, child_mask):
    group = lax.axis_index(GRP)
    z = lax.axis_index(Z)
    y = lax.axis_index("y")
    core = lax.axis_index("c")
    branch = group // 4
    grid = z * NY + y
    flat = group * (NZ * NY) + grid

    weight = lax.dynamic_slice_in_dim(child_mask, flat * SHARD, SHARD, 1).astype(f32)
    weight = jnp.repeat(weight.T, C, axis=1)
    own = jnp.pad(weight * child_factor, ((0, SLOT - SHARD), (0, 0)))

    below, above = shift_z(own, 4), shift_z(own, -4)

    s_sorted = spread_columns(s_parent)
    s_parts = exchange(s_sorted, ("c", "y"))
    near = jnp.concatenate([below, own, above], axis=0)
    low, high = shift_z(near, 1), shift_z(near, -1)
    far = shift_z(below, 4)
    low2 = shift_z(jnp.concatenate([low[0:64], far], axis=0), 1)
    high2 = shift_z(jnp.concatenate([high[32:96], far], axis=0), -1)
    pieces = (near, low, high, far, low2, high2)

    inverse = lax.dynamic_index_in_dim(panel_inverse, branch, 0, keepdims=False)

    inverse_cols = lax.dynamic_slice_in_dim(inverse, group % 4 * OWN, OWN, 1)
    kinds = lax.dynamic_index_in_dim(pivot_kind, branch, 0, keepdims=False)
    diags = lax.dynamic_index_in_dim(pivot_diag, branch, 0, keepdims=False)
    couples = lax.dynamic_index_in_dim(pivot_couple, branch, 0, keepdims=False)
    scaled = pivot_solve(inverse_cols, kinds, diags, couples)
    block = z % 4 * NY + y
    pivot_part = lax.dot_general(
        lax.dynamic_slice_in_dim(inverse, block * 32, 32, 1),
        scaled,
        (((0,), (0,)), ((), ())),
        precision=highest,
        preferred_element_type=f32,
    )
    pivot_part = jnp.where(lax.axis_index("h") == 0, pivot_part, 0.0)
    tile_weight = lax.dynamic_slice(child_mask, (branch, NY * ROWS * z), (1, NY * ROWS)).astype(f32)
    tile_weight = lax.dynamic_index_in_dim(tile_weight.reshape(NY, 2, NY, SHARD), y, 2, keepdims=False)
    tile_weight = jnp.pad(tile_weight, ((0, 0), (0, 0), (0, SLOT - SHARD))).reshape(PAD, 1)

    x = lax.axis_index("x")
    where = jnp.stack([z, core, x]).astype(jnp.int32)
    y_all, kept, *leaving = panel_rows(where, pieces, panel_inverse)
    y_all, s_parts = lax.optimization_barrier((y_all, s_parts))

    parts = [from_root(a, step) for a, step in zip(leaving, STEPS[1:])]
    image = chip_image(where, y_all, swap_core(y_all), s_parts)
    image, *parts = lax.optimization_barrier((image, *parts))
    got = exchange(image.reshape(32 * HALF, OWN), PLANE)
    mine = jnp.where(x == z // 4, kept, parts[0] + parts[1] + parts[2])
    y_rows = jnp.where(core == z // 2 % 2, mine, to_other_core(mine))

    off, term = finish(
        block.reshape(1).astype(jnp.int32), got.reshape(4, 2, NY, HALF, OWN), tile_weight, y_rows, pivot_part
    )

    rows = exchange(term, ("l", "y")).reshape(16, 32, OWN).sum(0)
    first = swap_y(jnp.concatenate([block_for(off, y ^ 2), block_for(off, y ^ 3)], axis=0), 2)
    rows, first = lax.optimization_barrier((rows, first))
    second = swap_y(jnp.concatenate([block_for(off, y ^ 1), first[2 * SLOT:]], axis=0), 1)
    rows = exchange(jnp.tile(rows, (4, 1)), "h").reshape(4, 32, OWN).sum(0)
    panel = exchange(jnp.tile(rows, (16, 1)), ("l", "y"))
    off = in_order(y.reshape(1).astype(jnp.int32), off, first, second)
    return off, panel


def solution(mesh):
    grid = Mesh(mesh.devices.reshape(4, 2, 4, 4, 4), AXES)
    lines = ("h", "l", "y")
    placed = (P(lines, GRP), P(AXES, None), P(), P(), P(), P(), P())
    return jax.shard_map(
        per_device,
        mesh=grid,
        in_specs=placed,
        out_specs=(P(lines, GRP), P(None, GRP)),
        check_vma=False,
    )
```

```python
import functools

import jax
import jax.numpy as jnp
import numpy as np
from jax import lax
from jax.experimental import pallas as pl
from jax.experimental.pallas import tpu as pltpu
from jax.sharding import Mesh
from jax.sharding import PartitionSpec as P

f32, bf16 = jnp.float32, jnp.bfloat16
highest = lax.Precision.HIGHEST

AXES = ("x", "c", "h", "l", "y")
Z = ("h", "l")
GRP = ("x", "c")
PLANE = ("x", "c", "y")
NZ, NY, NG = 16, 4, 8
SHARD = 30
SLOT = 32
ROWS = 240
PAD = 256
HALF = PAD // 2
COLS = 1920
WIDE = 1024
C = 512
OWN = 128
DEPTH = NZ * SLOT


def split2(a):
    hi = a.astype(bf16)
    return hi, (a - hi.astype(f32)).astype(bf16)


def dot3(ah, al, bh, bl):
    d = functools.partial(jnp.dot, preferred_element_type=f32)
    return d(ah, bh) + (d(ah, bl) + d(al, bh))


WINDOWS = [(480 * t // 128 * 128, -(-480 * (t + 1) // 128) * 128) for t in range(4)]


def sort_columns(s_any, out_any, s_ref, out_ref, in_sems, out_sems):
    loads = [
        pltpu.make_async_copy(
            s_any.at[:, pl.ds(begin, end - begin)], s_ref.at[t, :, pl.ds(0, end - begin)], in_sems.at[t]
        )
        for t, (begin, end) in enumerate(WINDOWS)
    ]
    stores = [
        pltpu.make_async_copy(
            out_ref.at[:, :, pl.ds(128 * t, 128)], out_any.at[:, :, pl.ds(128 * t, 128)], out_sems.at[t]
        )
        for t in range(4)
    ]
    for load in loads:
        load.start()
    for t, (begin, end) in enumerate(WINDOWS):
        row = lax.broadcasted_iota(jnp.int32, (end - begin, 512), 0)
        col = lax.broadcasted_iota(jnp.int32, (end - begin, 512), 1)
        part, place = col // 128, col % 128
        zz, i = place // SLOT, place % SLOT
        target = 480 * t - begin + 120 * zz + SHARD * part + i
        pick = jnp.where((row == target) & (i < SHARD), 1.0, 0.0).astype(bf16)
        loads[t].wait()
        hi, lo = split2(s_ref[t, :, :end - begin])
        got = jnp.dot(hi, pick, preferred_element_type=f32) + jnp.dot(
            lo, pick, preferred_element_type=f32
        )
        for q in range(NY):
            for k in range(8):
                part, begin, cols = k // 4 * NY + q, SLOT * (k % 4), slice(128 * t, 128 * t + 128)
                out_ref[part, begin:begin + SHARD, cols] = got[
                    SHARD * k:SHARD * (k + 1), 128 * q:128 * q + 128
                ]
                out_ref[part, begin + SHARD:begin + SLOT, cols] = jnp.zeros((SLOT - SHARD, 128), f32)
        stores[t].start()
    for store in stores:
        store.wait()


def spread_columns(s):
    anywhere = pl.BlockSpec(memory_space=pltpu.HBM)
    return pl.pallas_call(
        sort_columns,
        out_shape=jax.ShapeDtypeStruct((2 * NY, HALF, DEPTH), f32),
        in_specs=[anywhere],
        out_specs=anywhere,
        scratch_shapes=[
            pltpu.VMEM((4, ROWS, 640), f32),
            pltpu.VMEM((2 * NY, HALF, DEPTH), f32),
            pltpu.SemaphoreType.DMA((4,)),
            pltpu.SemaphoreType.DMA((4,)),
        ],
        compiler_params=pltpu.CompilerParams(vmem_limit_bytes=8 << 20),
        cost_estimate=pl.CostEstimate(
            flops=2 * 2 * ROWS * 640 * 512 * 4, bytes_accessed=4 * 2 * ROWS * 2048, transcendentals=0
        ),
    )(s)


PIECES = ((-4, 0, 4), (-5, -1, 3), (-3, 1, 5), (8,), (-6, -2, 7), (2, 6, 9))
N_PIECES = len(PIECES)


STEPS = (0, 2, 1, 3)


def panel_kernel(where_ref, *refs):
    pieces, (pinv_ref, y_ref, *own_refs, fac_ref) = refs[:N_PIECES], refs[N_PIECES:]
    z, core, x = where_ref[0], where_ref[1], where_ref[2]
    for ref, offsets in zip(pieces, PIECES):
        for k, offset in enumerate(offsets):
            slot = lax.rem(z + (1 - 2 * core) * offset + NZ, NZ)
            fac_ref[pl.ds(pl.multiple_of(slot * SLOT, SLOT), SLOT), :] = ref[SLOT * k:SLOT * (k + 1), :]
    for child in range(2):
        fh, fl = split2(fac_ref[:, C * child:C * (child + 1)])
        for j in range(2):
            ph, plo = split2(pinv_ref[child, :, 256 * j:256 * (j + 1)])
            begin = C * child + 256 * j
            y_ref[:, begin:begin + 256] = dot3(fh, fl, ph, plo)
    rows = pl.ds(pl.multiple_of(lax.rem(z, 2) * PAD, PAD), PAD)
    for step, out_ref in zip(STEPS, own_refs):
        child = lax.rem(x + step, 4) // 2
        out_ref[...] = y_ref[rows, pl.ds(pl.multiple_of(child * C, C), C)]


def panel_rows(where, pieces, pinv):
    vmem = pl.BlockSpec(memory_space=pltpu.VMEM)
    own = jax.ShapeDtypeStruct((PAD, C), f32)
    return pl.pallas_call(
        panel_kernel,
        out_shape=(jax.ShapeDtypeStruct((DEPTH, WIDE), f32),) + (own,) * 4,
        in_specs=[pl.BlockSpec(memory_space=pltpu.SMEM)] + [vmem] * (N_PIECES + 1),
        out_specs=(vmem,) * 5,
        scratch_shapes=[pltpu.VMEM((DEPTH, WIDE), f32)],
        compiler_params=pltpu.CompilerParams(vmem_limit_bytes=14 << 20),
        cost_estimate=pl.CostEstimate(
            flops=5 * 6 * DEPTH * WIDE * C, bytes_accessed=9 << 20, transcendentals=0
        ),
    )(where, *pieces, pinv)


def image_kernel(where_ref, y_ref, other_ref, s_ref, out_ref, sh_ref, sl_ref):
    core = where_ref[1]
    for side in range(2):
        first = NY * (core if side == 0 else 1 - core)
        sh, sl = split2(jnp.concatenate([s_ref[first + k] for k in range(NY)], axis=0))
        sh_ref[side] = sh
        sl_ref[side] = sl

    @pl.loop(0, WIDE // 256)
    def _(j):
        cols = pl.ds(pl.multiple_of(256 * j, 256), 256)
        u = dot3(sh_ref[0], sl_ref[0], *split2(y_ref[:, cols]))
        u = u + dot3(sh_ref[1], sl_ref[1], *split2(other_ref[:, cols]))
        for source in range(NY):
            for k in range(NY):
                begin = HALF * source + SLOT * k
                for g in range(2):
                    out_ref[2 * j + g, k, SLOT * source:SLOT * (source + 1), :] = u[
                        begin:begin + SLOT, OWN * g:OWN * (g + 1)
                    ]


def chip_image(where, y_rows, other, s_parts):
    vmem = pl.BlockSpec(memory_space=pltpu.VMEM)
    return pl.pallas_call(
        image_kernel,
        out_shape=jax.ShapeDtypeStruct((NG, NY, HALF, OWN), f32),
        in_specs=[pl.BlockSpec(memory_space=pltpu.SMEM)] + [vmem] * 3,
        out_specs=vmem,
        scratch_shapes=[pltpu.VMEM((2, NY * HALF, DEPTH), bf16), pltpu.VMEM((2, NY * HALF, DEPTH), bf16)],
        compiler_params=pltpu.CompilerParams(vmem_limit_bytes=16 << 20),
        cost_estimate=pl.CostEstimate(
            flops=12 * DEPTH * WIDE * NY * HALF, bytes_accessed=8 << 20, transcendentals=0
        ),
    )(where, y_rows, other, s_parts)


def finish_kernel(block_ref, got_ref, weight_ref, y_ref, pivot_ref, off_ref, term_ref):
    halves = []
    for core in range(2):
        total = got_ref[0, core, 0]
        for x in range(4):
            for y in range(NY):
                if x or y:
                    total = total + got_ref[x, core, y]
        halves.append(total)
    rows = [halves[core][SLOT * y:SLOT * (y + 1)] for y in range(NY) for core in range(2)]
    z_own = weight_ref[...] * jnp.concatenate(rows, axis=0)
    off_ref[...] = -z_own
    zh, zl = split2(z_own)
    yh, yl = split2(y_ref[...].T)
    term_ref[...] = dot3(yh, yl, zh, zl)
    mine = pl.ds(pl.multiple_of(32 * block_ref[0], 32), 32)
    term_ref[mine, :] += pivot_ref[...]


def finish(block, got, weight, y_rows, pivot):
    return pl.pallas_call(
        finish_kernel,
        out_shape=(
            jax.ShapeDtypeStruct((PAD, OWN), f32),
            jax.ShapeDtypeStruct((C, OWN), f32),
        ),
        in_specs=[pl.BlockSpec(memory_space=pltpu.SMEM)] + [pl.BlockSpec(memory_space=pltpu.VMEM)] * 4,
        compiler_params=pltpu.CompilerParams(vmem_limit_bytes=10 << 20),
        cost_estimate=pl.CostEstimate(
            flops=6 * C * PAD * OWN, bytes_accessed=4 << 20, transcendentals=0
        ),
    )(block, got, weight, y_rows, pivot)


def pivot_solve(inverse, pivot_kind, pivot_diag, pivot_couple):
    diag_next = jnp.roll(pivot_diag, -1)
    diag_prev = jnp.roll(pivot_diag, 1)
    couple_prev = jnp.roll(pivot_couple, 1)
    det_here = pivot_diag * diag_next - pivot_couple * pivot_couple
    det_prev = diag_prev * pivot_diag - couple_prev * couple_prev
    self_coef = jnp.where(
        pivot_kind == 0,
        1.0 / pivot_diag,
        jnp.where(pivot_kind == 1, diag_next / det_here, diag_prev / det_prev),
    )
    next_coef = jnp.where(pivot_kind == 1, -pivot_couple / det_here, 0.0)
    prev_coef = jnp.where(pivot_kind == 2, -couple_prev / det_prev, 0.0)
    inv_next = jnp.roll(inverse, -1, axis=0)
    inv_prev = jnp.roll(inverse, 1, axis=0)
    return (
        self_coef[:, None] * inverse + next_coef[:, None] * inv_next + prev_coef[:, None] * inv_prev
    )


def shift_z(a, step):
    pairs = [
        (core * NZ + z, core * NZ + (z + (1 - 2 * core) * step) % NZ) for core in range(2) for z in range(NZ)
    ]
    return lax.ppermute(a, ("c",) + Z, pairs)


def swap_core(a):
    return lax.ppermute(a, "c", [(0, 1), (1, 0)])


def place(x, core, z, y):
    return ((x * 2 + core) * NZ + z) * NY + y


def to_other_core(a):
    pairs = [
        (place(x, z // 2 % 2, z, y), place(x, 1 - z // 2 % 2, z, y))
        for x in range(4)
        for z in range(NZ)
        for y in range(NY)
    ]
    return lax.ppermute(a, AXES, pairs)


def from_root(a, step):
    pairs = [
        (place(z // 4, z // 2 % 2, z, y), place((z // 4 + step) % 4, z // 2 % 2, z, y))
        for z in range(NZ)
        for y in range(NY)
    ]
    return lax.ppermute(a, AXES, pairs)


def block_for(off, y):
    return lax.dynamic_slice_in_dim(off, y * 2 * SLOT, 2 * SLOT, 0)


def swap_y(a, bit):
    return lax.ppermute(a, "y", [(i, i ^ bit) for i in range(NY)])


def order_kernel(y_ref, off_ref, first_ref, second_ref, out_ref):
    y = y_ref[0]
    block = 2 * SLOT
    own = off_ref[pl.ds(pl.multiple_of(block * y, block), block), :]
    got = own, second_ref[:block], first_ref[:block], second_ref[block:]
    for source in range(NY):
        at = source ^ y
        rows = jnp.where(at == 0, got[0], jnp.where(at == 1, got[1], jnp.where(at == 2, got[2], got[3])))
        for k in range(2):
            begin = 120 * k + SHARD * source
            out_ref[begin:begin + SHARD, :] = rows[SLOT * k:SLOT * k + SHARD]


def in_order(y, off, first, second):
    vmem = pl.BlockSpec(memory_space=pltpu.VMEM)
    return pl.pallas_call(
        order_kernel,
        out_shape=jax.ShapeDtypeStruct((ROWS, OWN), f32),
        in_specs=[pl.BlockSpec(memory_space=pltpu.SMEM)] + [vmem] * 3,
        out_specs=vmem,
        compiler_params=pltpu.CompilerParams(vmem_limit_bytes=2 << 20),
    )(y, off, first, second)


def exchange(a, axes):
    return lax.all_to_all(a, axes, 0, 0, tiled=True)


def per_device(s_parent, child_factor, panel_inverse, pivot_kind, pivot_diag, pivot_couple, child_mask):
    group = lax.axis_index(GRP)
    z = lax.axis_index(Z)
    y = lax.axis_index("y")
    core = lax.axis_index("c")
    branch = group // 4
    grid = z * NY + y
    flat = group * (NZ * NY) + grid

    weight = lax.dynamic_slice_in_dim(child_mask, flat * SHARD, SHARD, 1).astype(f32)
    weight = jnp.repeat(weight.T, C, axis=1)
    own = jnp.pad(weight * child_factor, ((0, SLOT - SHARD), (0, 0)))

    below, above = shift_z(own, 4), shift_z(own, -4)

    s_sorted = spread_columns(s_parent)
    s_parts = exchange(s_sorted, ("c", "y"))
    near = jnp.concatenate([below, own, above], axis=0)
    low, high = shift_z(near, 1), shift_z(near, -1)
    far = shift_z(below, 4)
    low2 = shift_z(jnp.concatenate([low[0:64], far], axis=0), 1)
    high2 = shift_z(jnp.concatenate([high[32:96], far], axis=0), -1)
    pieces = (near, low, high, far, low2, high2)

    inverse = lax.dynamic_index_in_dim(panel_inverse, branch, 0, keepdims=False)

    inverse_cols = lax.dynamic_slice_in_dim(inverse, group % 4 * OWN, OWN, 1)
    kinds = lax.dynamic_index_in_dim(pivot_kind, branch, 0, keepdims=False)
    diags = lax.dynamic_index_in_dim(pivot_diag, branch, 0, keepdims=False)
    couples = lax.dynamic_index_in_dim(pivot_couple, branch, 0, keepdims=False)
    scaled = pivot_solve(inverse_cols, kinds, diags, couples)
    block = z % 4 * NY + y
    pivot_part = lax.dot_general(
        lax.dynamic_slice_in_dim(inverse, block * 32, 32, 1),
        scaled,
        (((0,), (0,)), ((), ())),
        precision=highest,
        preferred_element_type=f32,
    )
    pivot_part = jnp.where(lax.axis_index("h") == 0, pivot_part, 0.0)
    tile_weight = lax.dynamic_slice(child_mask, (branch, NY * ROWS * z), (1, NY * ROWS)).astype(f32)
    tile_weight = lax.dynamic_index_in_dim(tile_weight.reshape(NY, 2, NY, SHARD), y, 2, keepdims=False)
    tile_weight = jnp.pad(tile_weight, ((0, 0), (0, 0), (0, SLOT - SHARD))).reshape(PAD, 1)

    x = lax.axis_index("x")
    where = jnp.stack([z, core, x]).astype(jnp.int32)
    y_all, kept, *leaving = panel_rows(where, pieces, panel_inverse)
    y_all, s_parts = lax.optimization_barrier((y_all, s_parts))

    parts = [from_root(a, step) for a, step in zip(leaving, STEPS[1:])]
    image = chip_image(where, y_all, swap_core(y_all), s_parts)
    image, *parts = lax.optimization_barrier((image, *parts))
    got = exchange(image.reshape(32 * HALF, OWN), PLANE)
    mine = jnp.where(x == z // 4, kept, parts[0] + parts[1] + parts[2])
    y_rows = jnp.where(core == z // 2 % 2, mine, to_other_core(mine))

    off, term = finish(
        block.reshape(1).astype(jnp.int32), got.reshape(4, 2, NY, HALF, OWN), tile_weight, y_rows, pivot_part
    )

    rows = exchange(term, ("l", "y")).reshape(16, 32, OWN).sum(0)
    first = swap_y(jnp.concatenate([block_for(off, y ^ 2), block_for(off, y ^ 3)], axis=0), 2)
    rows, first = lax.optimization_barrier((rows, first))
    second = swap_y(jnp.concatenate([block_for(off, y ^ 1), first[2 * SLOT:]], axis=0), 1)
    rows = exchange(jnp.tile(rows, (4, 1)), "h").reshape(4, 32, OWN).sum(0)
    panel = exchange(jnp.tile(rows, (16, 1)), ("l", "y"))
    off = in_order(y.reshape(1).astype(jnp.int32), off, first, second)
    return off, panel


def solution(mesh):
    grid = Mesh(mesh.devices.reshape(4, 2, 4, 4, 4), AXES)
    lines = ("h", "l", "y")
    placed = (P(lines, GRP), P(AXES, None), P(), P(), P(), P(), P())
    return jax.shard_map(
        per_device,
        mesh=grid,
        in_specs=placed,
        out_specs=(P(lines, GRP), P(None, GRP)),
        check_vma=False,
    )
```

```python
import functools

import jax
import jax.numpy as jnp
import numpy as np
from jax import lax
from jax.experimental import pallas as pl
from jax.experimental.pallas import tpu as pltpu
from jax.sharding import Mesh
from jax.sharding import PartitionSpec as P

f32, bf16 = jnp.float32, jnp.bfloat16
highest = lax.Precision.HIGHEST

AXES = ("x", "c", "h", "l", "y")
Z = ("h", "l")
GRP = ("x", "c")
PLANE = ("x", "c", "y")
NZ, NY, NG = 16, 4, 8
SHARD = 30
SLOT = 32
ROWS = 240
PAD = 256
HALF = PAD // 2
COLS = 1920
WIDE = 1024
C = 512
OWN = 128
DEPTH = NZ * SLOT


def split2(a):
    hi = a.astype(bf16)
    return hi, (a - hi.astype(f32)).astype(bf16)


def dot3(ah, al, bh, bl):
    d = functools.partial(jnp.dot, preferred_element_type=f32)
    return d(ah, bh) + (d(ah, bl) + d(al, bh))


WINDOWS = [(480 * t // 128 * 128, -(-480 * (t + 1) // 128) * 128) for t in range(4)]


def sort_columns(s_any, out_any, s_ref, out_ref, in_sems, out_sems):
    loads = [
        pltpu.make_async_copy(
            s_any.at[:, pl.ds(begin, end - begin)], s_ref.at[t, :, pl.ds(0, end - begin)], in_sems.at[t]
        )
        for t, (begin, end) in enumerate(WINDOWS)
    ]
    stores = [
        pltpu.make_async_copy(
            out_ref.at[:, :, pl.ds(128 * t, 128)], out_any.at[:, :, pl.ds(128 * t, 128)], out_sems.at[t]
        )
        for t in range(4)
    ]
    for load in loads:
        load.start()
    for t, (begin, end) in enumerate(WINDOWS):
        row = lax.broadcasted_iota(jnp.int32, (end - begin, 512), 0)
        col = lax.broadcasted_iota(jnp.int32, (end - begin, 512), 1)
        part, place = col // 128, col % 128
        zz, i = place // SLOT, place % SLOT
        target = 480 * t - begin + 120 * zz + SHARD * part + i
        pick = jnp.where((row == target) & (i < SHARD), 1.0, 0.0).astype(bf16)
        loads[t].wait()
        hi, lo = split2(s_ref[t, :, :end - begin])
        got = jnp.dot(hi, pick, preferred_element_type=f32) + jnp.dot(
            lo, pick, preferred_element_type=f32
        )
        for q in range(NY):
            for k in range(8):
                part, begin, cols = k // 4 * NY + q, SLOT * (k % 4), slice(128 * t, 128 * t + 128)
                out_ref[part, begin:begin + SHARD, cols] = got[
                    SHARD * k:SHARD * (k + 1), 128 * q:128 * q + 128
                ]
                out_ref[part, begin + SHARD:begin + SLOT, cols] = jnp.zeros((SLOT - SHARD, 128), f32)
        stores[t].start()
    for store in stores:
        store.wait()


def spread_columns(s):
    anywhere = pl.BlockSpec(memory_space=pltpu.HBM)
    return pl.pallas_call(
        sort_columns,
        out_shape=jax.ShapeDtypeStruct((2 * NY, HALF, DEPTH), f32),
        in_specs=[anywhere],
        out_specs=anywhere,
        scratch_shapes=[
            pltpu.VMEM((4, ROWS, 640), f32),
            pltpu.VMEM((2 * NY, HALF, DEPTH), f32),
            pltpu.SemaphoreType.DMA((4,)),
            pltpu.SemaphoreType.DMA((4,)),
        ],
        compiler_params=pltpu.CompilerParams(vmem_limit_bytes=8 << 20),
        cost_estimate=pl.CostEstimate(
            flops=2 * 2 * ROWS * 640 * 512 * 4, bytes_accessed=4 * 2 * ROWS * 2048, transcendentals=0
        ),
    )(s)


PIECES = ((-4, 0, 4), (-5, -1, 3), (-3, 1, 5), (8,), (-6, -2, 7), (2, 6, 9))
N_PIECES = len(PIECES)


STEPS = (2, 1, 3)


def panel_kernel(where_ref, *refs):
    pieces, (pinv_ref, y_ref, *own_refs, fac_ref) = refs[:N_PIECES], refs[N_PIECES:]
    z, core, x = where_ref[0], where_ref[1], where_ref[2]
    for ref, offsets in zip(pieces, PIECES):
        for k, offset in enumerate(offsets):
            slot = lax.rem(z + (1 - 2 * core) * offset + NZ, NZ)
            fac_ref[pl.ds(pl.multiple_of(slot * SLOT, SLOT), SLOT), :] = ref[SLOT * k:SLOT * (k + 1), :]
    for child in range(2):
        fh, fl = split2(fac_ref[:, C * child:C * (child + 1)])
        for j in range(2):
            ph, plo = split2(pinv_ref[child, :, 256 * j:256 * (j + 1)])
            begin = C * child + 256 * j
            y_ref[:, begin:begin + 256] = dot3(fh, fl, ph, plo)
    rows = pl.ds(pl.multiple_of(lax.rem(z, 2) * PAD, PAD), PAD)
    for step, out_ref in zip(STEPS, own_refs):
        child = lax.rem(x + step, 4) // 2
        out_ref[...] = y_ref[rows, pl.ds(pl.multiple_of(child * C, C), C)]


def panel_rows(where, pieces, pinv):
    vmem = pl.BlockSpec(memory_space=pltpu.VMEM)
    own = jax.ShapeDtypeStruct((PAD, C), f32)
    return pl.pallas_call(
        panel_kernel,
        out_shape=(jax.ShapeDtypeStruct((DEPTH, WIDE), f32),) + (own,) * 3,
        in_specs=[pl.BlockSpec(memory_space=pltpu.SMEM)] + [vmem] * (N_PIECES + 1),
        out_specs=(vmem,) * 4,
        scratch_shapes=[pltpu.VMEM((DEPTH, WIDE), f32)],
        compiler_params=pltpu.CompilerParams(vmem_limit_bytes=14 << 20),
        cost_estimate=pl.CostEstimate(
            flops=5 * 6 * DEPTH * WIDE * C, bytes_accessed=9 << 20, transcendentals=0
        ),
    )(where, *pieces, pinv)


def image_kernel(where_ref, y_ref, other_ref, s_ref, out_ref, sh_ref, sl_ref):
    core = where_ref[1]
    for side in range(2):
        first = NY * (core if side == 0 else 1 - core)
        sh, sl = split2(jnp.concatenate([s_ref[first + k] for k in range(NY)], axis=0))
        sh_ref[side] = sh
        sl_ref[side] = sl

    @pl.loop(0, WIDE // 256)
    def _(j):
        cols = pl.ds(pl.multiple_of(256 * j, 256), 256)
        u = dot3(sh_ref[0], sl_ref[0], *split2(y_ref[:, cols]))
        u = u + dot3(sh_ref[1], sl_ref[1], *split2(other_ref[:, cols]))
        for source in range(NY):
            for k in range(NY):
                begin = HALF * source + SLOT * k
                for g in range(2):
                    out_ref[2 * j + g, k, SLOT * source:SLOT * (source + 1), :] = u[
                        begin:begin + SLOT, OWN * g:OWN * (g + 1)
                    ]


def chip_image(where, y_rows, other, s_parts):
    vmem = pl.BlockSpec(memory_space=pltpu.VMEM)
    return pl.pallas_call(
        image_kernel,
        out_shape=jax.ShapeDtypeStruct((NG, NY, HALF, OWN), f32),
        in_specs=[pl.BlockSpec(memory_space=pltpu.SMEM)] + [vmem] * 3,
        out_specs=vmem,
        scratch_shapes=[pltpu.VMEM((2, NY * HALF, DEPTH), bf16), pltpu.VMEM((2, NY * HALF, DEPTH), bf16)],
        compiler_params=pltpu.CompilerParams(vmem_limit_bytes=16 << 20),
        cost_estimate=pl.CostEstimate(
            flops=12 * DEPTH * WIDE * NY * HALF, bytes_accessed=8 << 20, transcendentals=0
        ),
    )(where, y_rows, other, s_parts)


def finish_kernel(block_ref, got_ref, weight_ref, y_ref, pivot_ref, off_ref, term_ref):
    halves = []
    for core in range(2):
        total = got_ref[0, core, 0]
        for x in range(4):
            for y in range(NY):
                if x or y:
                    total = total + got_ref[x, core, y]
        halves.append(total)
    rows = [halves[core][SLOT * y:SLOT * (y + 1)] for y in range(NY) for core in range(2)]
    z_own = weight_ref[...] * jnp.concatenate(rows, axis=0)
    off_ref[...] = -z_own
    zh, zl = split2(z_own)
    yh, yl = split2(y_ref[...].T)
    term_ref[...] = dot3(yh, yl, zh, zl)
    mine = pl.ds(pl.multiple_of(32 * block_ref[0], 32), 32)
    term_ref[mine, :] += pivot_ref[...]


def finish(block, got, weight, y_rows, pivot):
    return pl.pallas_call(
        finish_kernel,
        out_shape=(
            jax.ShapeDtypeStruct((PAD, OWN), f32),
            jax.ShapeDtypeStruct((C, OWN), f32),
        ),
        in_specs=[pl.BlockSpec(memory_space=pltpu.SMEM)] + [pl.BlockSpec(memory_space=pltpu.VMEM)] * 4,
        compiler_params=pltpu.CompilerParams(vmem_limit_bytes=10 << 20),
        cost_estimate=pl.CostEstimate(
            flops=6 * C * PAD * OWN, bytes_accessed=4 << 20, transcendentals=0
        ),
    )(block, got, weight, y_rows, pivot)


def pivot_solve(inverse, pivot_kind, pivot_diag, pivot_couple):
    diag_next = jnp.roll(pivot_diag, -1)
    diag_prev = jnp.roll(pivot_diag, 1)
    couple_prev = jnp.roll(pivot_couple, 1)
    det_here = pivot_diag * diag_next - pivot_couple * pivot_couple
    det_prev = diag_prev * pivot_diag - couple_prev * couple_prev
    self_coef = jnp.where(
        pivot_kind == 0,
        1.0 / pivot_diag,
        jnp.where(pivot_kind == 1, diag_next / det_here, diag_prev / det_prev),
    )
    next_coef = jnp.where(pivot_kind == 1, -pivot_couple / det_here, 0.0)
    prev_coef = jnp.where(pivot_kind == 2, -couple_prev / det_prev, 0.0)
    inv_next = jnp.roll(inverse, -1, axis=0)
    inv_prev = jnp.roll(inverse, 1, axis=0)
    return (
        self_coef[:, None] * inverse + next_coef[:, None] * inv_next + prev_coef[:, None] * inv_prev
    )


def shift_z(a, step):
    pairs = [
        (core * NZ + z, core * NZ + (z + (1 - 2 * core) * step) % NZ) for core in range(2) for z in range(NZ)
    ]
    return lax.ppermute(a, ("c",) + Z, pairs)


def swap_core(a):
    return lax.ppermute(a, "c", [(0, 1), (1, 0)])


def place(x, core, z, y):
    return ((x * 2 + core) * NZ + z) * NY + y


def to_other_core(a):
    pairs = [
        (place(x, z // 2 % 2, z, y), place(x, 1 - z // 2 % 2, z, y))
        for x in range(4)
        for z in range(NZ)
        for y in range(NY)
    ]
    return lax.ppermute(a, AXES, pairs)


def from_root(a, step):
    pairs = [
        (place(z // 4, z // 2 % 2, z, y), place((z // 4 + step) % 4, z // 2 % 2, z, y))
        for z in range(NZ)
        for y in range(NY)
    ]
    return lax.ppermute(a, AXES, pairs)


def block_for(off, y):
    return lax.dynamic_slice_in_dim(off, y * 2 * SLOT, 2 * SLOT, 0)


def swap_y(a, bit):
    return lax.ppermute(a, "y", [(i, i ^ bit) for i in range(NY)])


def order_kernel(y_ref, off_ref, first_ref, second_ref, out_ref):
    y = y_ref[0]
    block = 2 * SLOT
    own = off_ref[pl.ds(pl.multiple_of(block * y, block), block), :]
    got = own, second_ref[:block], first_ref[:block], second_ref[block:]
    for source in range(NY):
        at = source ^ y
        rows = jnp.where(at == 0, got[0], jnp.where(at == 1, got[1], jnp.where(at == 2, got[2], got[3])))
        for k in range(2):
            begin = 120 * k + SHARD * source
            out_ref[begin:begin + SHARD, :] = rows[SLOT * k:SLOT * k + SHARD]


def in_order(y, off, first, second):
    vmem = pl.BlockSpec(memory_space=pltpu.VMEM)
    return pl.pallas_call(
        order_kernel,
        out_shape=jax.ShapeDtypeStruct((ROWS, OWN), f32),
        in_specs=[pl.BlockSpec(memory_space=pltpu.SMEM)] + [vmem] * 3,
        out_specs=vmem,
        compiler_params=pltpu.CompilerParams(vmem_limit_bytes=2 << 20),
    )(y, off, first, second)


def exchange(a, axes):
    return lax.all_to_all(a, axes, 0, 0, tiled=True)


def per_device(s_parent, child_factor, panel_inverse, pivot_kind, pivot_diag, pivot_couple, child_mask):
    group = lax.axis_index(GRP)
    z = lax.axis_index(Z)
    y = lax.axis_index("y")
    core = lax.axis_index("c")
    branch = group // 4
    grid = z * NY + y
    flat = group * (NZ * NY) + grid

    weight = lax.dynamic_slice_in_dim(child_mask, flat * SHARD, SHARD, 1).astype(f32)
    weight = jnp.repeat(weight.T, C, axis=1)
    own = jnp.pad(weight * child_factor, ((0, SLOT - SHARD), (0, 0)))

    below, above = shift_z(own, 4), shift_z(own, -4)

    s_sorted = spread_columns(s_parent)
    s_parts = exchange(s_sorted, ("c", "y"))
    near = jnp.concatenate([below, own, above], axis=0)
    low, high = shift_z(near, 1), shift_z(near, -1)
    far = shift_z(below, 4)
    low2 = shift_z(jnp.concatenate([low[0:64], far], axis=0), 1)
    high2 = shift_z(jnp.concatenate([high[32:96], far], axis=0), -1)
    pieces = (near, low, high, far, low2, high2)

    inverse = lax.dynamic_index_in_dim(panel_inverse, branch, 0, keepdims=False)

    inverse_cols = lax.dynamic_slice_in_dim(inverse, group % 4 * OWN, OWN, 1)
    kinds = lax.dynamic_index_in_dim(pivot_kind, branch, 0, keepdims=False)
    diags = lax.dynamic_index_in_dim(pivot_diag, branch, 0, keepdims=False)
    couples = lax.dynamic_index_in_dim(pivot_couple, branch, 0, keepdims=False)
    scaled = pivot_solve(inverse_cols, kinds, diags, couples)
    block = z % 4 * NY + y
    pivot_part = lax.dot_general(
        lax.dynamic_slice_in_dim(inverse, block * 32, 32, 1),
        scaled,
        (((0,), (0,)), ((), ())),
        precision=highest,
        preferred_element_type=f32,
    )
    pivot_part = jnp.where(lax.axis_index("h") == 0, pivot_part, 0.0)
    tile_weight = lax.dynamic_slice(child_mask, (branch, NY * ROWS * z), (1, NY * ROWS)).astype(f32)
    tile_weight = lax.dynamic_index_in_dim(tile_weight.reshape(NY, 2, NY, SHARD), y, 2, keepdims=False)
    tile_weight = jnp.pad(tile_weight, ((0, 0), (0, 0), (0, SLOT - SHARD))).reshape(PAD, 1)

    x = lax.axis_index("x")
    where = jnp.stack([z, core, x]).astype(jnp.int32)
    y_all, *leaving = panel_rows(where, pieces, panel_inverse)
    y_all, s_parts = lax.optimization_barrier((y_all, s_parts))

    parts = [from_root(a, step) for a, step in zip(leaving, STEPS)]
    image = chip_image(where, y_all, swap_core(y_all), s_parts)
    image, *parts = lax.optimization_barrier((image, *parts))
    got = exchange(image.reshape(32 * HALF, OWN), PLANE)
    kept = jnp.where(x % 2 == 0, leaving[1], leaving[2])
    mine = jnp.where(x == z // 4, kept, parts[0] + parts[1] + parts[2])
    y_rows = jnp.where(core == z // 2 % 2, mine, to_other_core(mine))

    off, term = finish(
        block.reshape(1).astype(jnp.int32), got.reshape(4, 2, NY, HALF, OWN), tile_weight, y_rows, pivot_part
    )

    rows = exchange(term, ("l", "y")).reshape(16, 32, OWN).sum(0)
    first = swap_y(jnp.concatenate([block_for(off, y ^ 2), block_for(off, y ^ 3)], axis=0), 2)
    rows, first = lax.optimization_barrier((rows, first))
    second = swap_y(jnp.concatenate([block_for(off, y ^ 1), first[2 * SLOT:]], axis=0), 1)
    rows = exchange(jnp.tile(rows, (4, 1)), "h").reshape(4, 32, OWN).sum(0)
    panel = exchange(jnp.tile(rows, (16, 1)), ("l", "y"))
    off = in_order(y.reshape(1).astype(jnp.int32), off, first, second)
    return off, panel


def solution(mesh):
    grid = Mesh(mesh.devices.reshape(4, 2, 4, 4, 4), AXES)
    lines = ("h", "l", "y")
    placed = (P(lines, GRP), P(AXES, None), P(), P(), P(), P(), P())
    return jax.shard_map(
        per_device,
        mesh=grid,
        in_specs=placed,
        out_specs=(P(lines, GRP), P(None, GRP)),
        check_vma=False,
    )
```
